32 devices in a mesh: groups: 2 (over y), tensor: 4 (over z), dp: 2 (over x), seq: 2 (over core).
Axes of the slice: x: 2, y: 2, z: 4, core: 2. Of those that a mesh axis runs over, the one named last changes fastest.
Arguments:
- out_grad: bfloat16 [4096, 4096], P(('groups', 'dp', 'seq'), 'tensor'), parts along dimension 0, may hold values from -6 to 6
- layer_in: bfloat16 [4096, 4096], P(('groups', 'dp', 'seq'), 'tensor'), parts along dimension 0, may hold values from -6 to 6
- gate_pre: bfloat16 [4096, 14336], P(('groups', 'dp', 'seq'), 'tensor'), parts along dimension 0, may hold values from -8 to 8
- down_weight: bfloat16 [14336, 4096], P('tensor'), may hold values from -0.09375 to 0.09375
- proj_in: bfloat16 [4096, 64], P('tensor'), may hold values from -0.09375 to 0.09375
- proj_out: bfloat16 [14336, 64], P('tensor'), may hold values from -0.046875 to 0.046875
- segment_ids: int32 [4, 1024], P(('groups', 'dp'), 'seq'), parts along dimension 0, may hold values from 0 to 3, never falling along the last dimension, each value on 1 to 512 neighbouring positions
- query_bank: bfloat16 [256, 4096], P(('groups', 'dp')), parts along dimension 0, may hold values from -6 to 6
- query_ids: int32 [512], P('groups'), parts along dimension 0, may hold values from 0 to 127
Outputs:
- scores: float32 [16, 256], P(('groups', 'dp')), parts along dimension 0
The draws below stay inside these ranges and needn't reach their ends.
There are 2 independent parts, one for each index of `groups`. The reference program is written for one: setup_inputs(seed, part) draws one part's arguments, and reference() takes and returns one part's arrays. A program takes and returns all parts, laid end to end along the dimension named above; an argument that names none is the same for every part. Nothing has to cross between parts.
Inputs may be any that keep to these rules, and one draw needn't show every extreme that they name: `segment_ids`: ids never fall along a row; every id of a row occurs; one example of a row has exactly 512 tokens.
All inputs are finite; a program needn't handle non-finite values.
Results may differ from the reference program's by a relative error of at most 0.003.
Values may be sent and summed in bfloat16 or wider, within the bound.
No kernel may reach another device: no remote copies, remote signals or barrier semaphores. Data moves between devices by JAX's collectives and lax.ppermute only.
A program may use at most 128 MiB of HBM per device.

```python
import math
import jax
import jax.numpy as jnp
import numpy as np
from jax import lax

D = 4096
FF = 14336
K = 64
KK = 4096
SPAN = 1024
TOKENS = 2048
EX_DEV = 4
EXAMPLES = 8
QBANK = 128
QUERIES = 256
N_DP = 2


def place_ends(values, own_key, low, largest):
    longest = values.shape.index(max(values.shape))
    spots = []
    for shift in (0, 1):
        where = [jax.random.randint(jax.random.fold_in(own_key, axis), (), 0, length) for axis, length in enumerate(values.shape)]
        where[longest] = (where[longest] + shift) % values.shape[longest]
        spots.append(tuple(where))
    return values.at[spots[0]].set(low).at[spots[1]].set(largest)


def levels(key, extent, pieces, low, largest):
    gain = 1.0
    for position, parts in pieces:
        heights = jax.random.uniform(jax.random.fold_in(jax.random.fold_in(key, 6), position), (parts,), jnp.float32, low / len(pieces), largest / len(pieces))
        gain = gain * jnp.repeat(jnp.exp(heights), extent[position] // parts).reshape((-1,) + (1,) * (len(extent) - 1 - position))
    return gain


def length_profile(number_of, total, bound, lean):
    weights = [(1 << 20) // math.isqrt(grade ** lean) + 1 for grade in range(2, number_of + 1)]
    spare, given = total - bound - (number_of - 1), [1] * (number_of - 1)
    while spare > 0:
        candidates = [i for i in range(number_of - 1) if given[i] < bound]
        pool, budget = sum([weights[i] for i in candidates]), spare
        for i in candidates:
            more = min(bound - given[i], max(1, budget * weights[i] // pool), spare)
            given[i] = given[i] + more
            spare = spare - more
    return np.array([bound] + given)


def uneven(own_key, amount, total, reach, skew):
    if amount == 2:
        one = jax.random.randint(own_key, (), max(1, total - reach), min(reach, total - 1) + 1)
        return jnp.stack([one, total - one])
    tallies = jnp.asarray(length_profile(amount, total, reach, skew), jnp.int32)
    twos = (amount - 1) // 2
    giver, taker = tallies[1:1 + 2 * twos:2], tallies[2:2 + 2 * twos:2]
    room = jnp.minimum(giver - 1, reach - taker)
    shifted = jax.random.randint(jax.random.fold_in(own_key, 1), (twos,), 0, 1 << 20) % (room + 1)
    tallies = tallies.at[1:1 + 2 * twos:2].set(giver - shifted).at[2:2 + 2 * twos:2].set(taker + shifted)
    return tallies[jax.random.permutation(jax.random.fold_in(own_key, 2), amount)]


def scatter_about(own_key, shape, deviation, bound, pieces=(), kind=jnp.bfloat16):
    entries = deviation * jax.random.normal(own_key, shape, jnp.float32)
    if pieces:
        entries = entries * levels(own_key, shape, pieces, -0.22, 0.18)
    return jnp.clip(entries, -bound, bound).astype(kind)


def setup_inputs(seed: int = 0, part: int = 0) -> dict:
    seeds = jax.random.split(jax.random.key(seed), 10)
    part_splits = jax.random.split(jax.random.fold_in(seeds[9], part), 10)
    return {
        "out_grad": scatter_about(part_splits[0], (TOKENS, D), 1.0, 6.0, ((0, 4), (1, 4))),
        "layer_in": scatter_about(part_splits[1], (TOKENS, D), 1.0, 6.0, ((0, 4), (1, 4))),
        "gate_pre": scatter_about(part_splits[2], (TOKENS, FF), 1.5, 8.0, ((0, 4), (1, 4))),
        "down_weight": scatter_about(seeds[3], (FF, D), D ** -0.5, 0.09375, ((0, 4),)),
        "proj_in": scatter_about(seeds[4], (D, K), D ** -0.5, 0.09375, ((0, 4),)),
        "proj_out": scatter_about(seeds[5], (FF, K), FF ** -0.5, 0.046875, ((0, 4),)),
        "segment_ids": jax.vmap(lambda own: jnp.searchsorted(jnp.cumsum(uneven(own, EX_DEV, SPAN, SPAN // 2, 1)), jnp.arange(SPAN), side="right"))(jax.random.split(part_splits[6], N_DP)).reshape((N_DP, SPAN)).astype(jnp.int32),
        "query_bank": scatter_about(part_splits[7], (QBANK, KK), 1.0, 6.0, ((0, 2),)),
        "query_ids": place_ends(jax.random.randint(part_splits[8], (QUERIES,), 0, QBANK), jax.random.fold_in(part_splits[8], 1), 0, QBANK - 1).astype(jnp.int32),
    }


exact_precision = lax.Precision.HIGHEST


def reference(out_grad, layer_in, gate_pre, down_weight, proj_in, proj_out, segment_ids, query_bank, query_ids):
    hidden_grad = jnp.dot(out_grad.astype(jnp.float32), down_weight.astype(jnp.float32).T, precision=exact_precision)
    up_grad = (hidden_grad * jax.nn.silu(gate_pre.astype(jnp.float32))).astype(jnp.bfloat16)
    in_sketch = jnp.dot(layer_in.astype(jnp.float32), proj_in.astype(jnp.float32), precision=exact_precision)
    out_sketch = jnp.dot(up_grad.astype(jnp.float32), proj_out.astype(jnp.float32), precision=exact_precision)
    owners = (segment_ids + jnp.arange(N_DP, dtype=jnp.int32)[:, None] * EX_DEV).reshape(-1)
    onehot = (owners[:, None] == jnp.arange(EXAMPLES, dtype=jnp.int32)[None, :]).astype(jnp.float32)
    weighted = (onehot[:, :, None] * out_sketch[:, None, :]).reshape(TOKENS, EXAMPLES * K)
    sketch = lax.dot_general(weighted, in_sketch, (((0,), (0,)), ((), ())), precision=exact_precision)
    sketch = sketch.reshape(EXAMPLES, KK)
    picked = query_bank[query_ids].astype(jnp.float32)
    scores = jnp.dot(sketch, picked.T, precision=exact_precision)
    return scores * (1.0 / (8.0 * K))
```

```python
import functools

import jax
import jax.numpy as jnp
from jax import lax
from jax.experimental import pallas as pl
from jax.experimental.pallas import tpu as pltpu
from jax.sharding import PartitionSpec as P

EX_DEV = 4
EXACT = lax.Precision.HIGHEST
NT = (((1,), (1,)), ((), ()))


def after(value, *deps):
    return lax.optimization_barrier((value, *deps))[0]


def sum_over(value, axis, size):
    step = 1
    while step < size:
        value = value + lax.ppermute(value, axis, [(i, i ^ step) for i in range(size)])
        step *= 2
    return value


def tile_of(count, largest):
    return max((t for t in range(128, largest + 1, 128) if count % t == 0), default=count)


def hidden_kernel(blocks, place_ref, *refs):
    parts, weights, total_ref = refs[:blocks], refs[blocks : 2 * blocks], refs[-1]
    total = lax.dot_general(parts[0][...], weights[0][...], NT, preferred_element_type=jnp.float32)
    for part, weight in zip(parts[1:], weights[1:]):
        total += lax.dot_general(part[...], weight[...], NT, preferred_element_type=jnp.float32)
    total_ref[...] = total


def hidden_sum(parts, places, weight):
    tokens, width = parts[0].shape
    hidden = weight.shape[0]
    tile = tile_of(hidden, 512)
    blocks = len(parts)
    return pl.pallas_call(
        functools.partial(hidden_kernel, blocks),
        grid_spec=pltpu.PrefetchScalarGridSpec(
            num_scalar_prefetch=1,
            grid=(hidden // tile,),
            in_specs=[pl.BlockSpec((tokens, width), lambda f, place: (0, 0))] * blocks
            + [pl.BlockSpec((tile, width), lambda f, place, k=k: (f, place[k])) for k in range(blocks)],
            out_specs=pl.BlockSpec((tokens, tile), lambda f, place: (0, f)),
        ),
        out_shape=jax.ShapeDtypeStruct((tokens, hidden), jnp.float32),
        compiler_params=pltpu.CompilerParams(vmem_limit_bytes=24 << 20),
        cost_estimate=pl.CostEstimate(
            flops=2 * blocks * tokens * width * hidden,
            bytes_accessed=2 * blocks * width * (tokens + hidden) + 4 * tokens * hidden,
            transcendentals=0,
        ),
    )(places, *parts, *([weight] * blocks))


def last_kernel(
    scale, place_ref, part_ref, weight_ref, total_ref, gate_ref, proj_ref, inside_ref, bank_ref, pick_ref,
    scores_ref, out_ref, sketch_ref, flat_ref,
):
    step = pl.program_id(0)
    hidden = total_ref[...] + lax.dot_general(
        part_ref[...], weight_ref[...], NT, preferred_element_type=jnp.float32
    )
    gate = gate_ref[...].astype(jnp.float32)
    up = (hidden * (gate / (1.0 + jnp.exp(-gate)))).astype(jnp.bfloat16)
    term = jnp.dot(up, proj_ref[...], preferred_element_type=jnp.float32)

    @pl.when(step == 0)
    def _():
        out_ref[...] = term

    @pl.when(step > 0)
    def _():
        out_ref[...] += term

    @pl.when(step == pl.num_programs(0) - 1)
    def _():
        rows = inside_ref.shape[0] // EX_DEV
        half = out_ref.shape[1] // 2
        sketch_ref[...] = jnp.dot(
            inside_ref[...], out_ref[...], precision=EXACT, preferred_element_type=jnp.float32
        )
        left = lax.broadcasted_iota(jnp.int32, (EX_DEV, 2 * half), 1) < half
        for pair in range(rows // 2):
            first = sketch_ref[pl.ds(2 * pair, EX_DEV, stride=rows), :]
            second = sketch_ref[pl.ds(2 * pair + 1, EX_DEV, stride=rows), :]
            flat_ref[:, 2 * half * pair : 2 * half * (pair + 1)] = jnp.where(left, first, second)
        flat = flat_ref[...]
        high = flat.astype(jnp.bfloat16)
        rest = flat - high.astype(jnp.float32)
        mid = rest.astype(jnp.bfloat16)
        low = (rest - mid.astype(jnp.float32)).astype(jnp.bfloat16)
        bank = bank_ref[...]
        found = sum(lax.dot_general(t, bank, NT, preferred_element_type=jnp.float32) for t in (high, mid, low))
        scores_ref[...] = scale * jnp.dot(
            found, pick_ref[...], precision=EXACT, preferred_element_type=jnp.float32
        )


def last_scores(part, place, weight, total, gate, proj, inside, bank, pick, scale):
    tokens, width = part.shape
    hidden = weight.shape[0]
    tile = tile_of(hidden, 512)
    whole = lambda a: pl.BlockSpec(a.shape, lambda f, place: (0,) * a.ndim)
    return pl.pallas_call(
        functools.partial(last_kernel, scale),
        grid_spec=pltpu.PrefetchScalarGridSpec(
            num_scalar_prefetch=1,
            grid=(hidden // tile,),
            in_specs=[
                whole(part),
                pl.BlockSpec((tile, width), lambda f, place: (f, place[0])),
                pl.BlockSpec((tokens, tile), lambda f, place: (0, f)),
                pl.BlockSpec((tokens, tile), lambda f, place: (0, f)),
                pl.BlockSpec((tile, proj.shape[1]), lambda f, place: (f, 0)),
                whole(inside),
                whole(bank),
                whole(pick),
            ],
            out_specs=pl.BlockSpec((EX_DEV, pick.shape[1]), lambda f, place: (0, 0)),
            scratch_shapes=[
                pltpu.VMEM((tokens, proj.shape[1]), jnp.float32),
                pltpu.VMEM((inside.shape[0], proj.shape[1]), jnp.float32),
                pltpu.VMEM((EX_DEV, bank.shape[1]), jnp.float32),
            ],
        ),
        out_shape=jax.ShapeDtypeStruct((EX_DEV, pick.shape[1]), jnp.float32),
        compiler_params=pltpu.CompilerParams(vmem_limit_bytes=28 << 20),
        cost_estimate=pl.CostEstimate(
            flops=2 * tokens * width * hidden,
            bytes_accessed=2 * width * (tokens + hidden) + 6 * tokens * hidden,
            transcendentals=tokens * hidden,
        ),
    )(place, part, weight, total, gate, proj, inside, bank, pick)


def whole_bank(query_bank, query_ids, size):
    me = lax.axis_index("dp")
    held = query_bank.shape[0]
    rows = jnp.arange(held, dtype=jnp.int32)
    parts, places = [query_bank], [me * held + rows]
    for k in range(1, size):
        parts.append(lax.ppermute(query_bank, "dp", [(i, (i + k) % size) for i in range(size)]))
        places.append((me - k) % size * held + rows)
    pick = (jnp.concatenate(places)[:, None] == query_ids[None, :]).astype(jnp.float32)
    return jnp.concatenate(parts), pick


def body(
    sizes, out_grad, layer_in, gate_pre, down_weight, proj_in, proj_out, segment_ids, query_bank, query_ids
):
    tensor = sizes["tensor"]
    me = lax.axis_index("tensor")
    width = proj_in.shape[1]
    scale = 1.0 / (8.0 * width)

    send = lambda value, pairs: lax.ppermute(value, "tensor", pairs)
    if tensor == 4:
        near = send(out_grad, [(0, 1), (1, 0), (2, 3), (3, 2)])
        middle = send(out_grad, [(1, 2), (2, 1), (0, 0), (3, 3)])
        cross = send(out_grad, [(0, 3), (3, 0)])
        far = send(middle, [(0, 2), (2, 3), (3, 1), (1, 0)])
        rest = jnp.where((me == 0) | (me == 3), cross, middle)
        parts = [out_grad, near, far]
        pick_of = lambda *t: jnp.asarray(t, jnp.int32)[me]
        places = jnp.stack([me, me ^ 1, pick_of(2, 3, 0, 1)]).astype(jnp.int32)
        place = pick_of(3, 2, 1, 0)[None]
    else:
        gathered = lax.all_gather(out_grad, "tensor", axis=1, tiled=True)
        step = gathered.shape[1] // 2
        parts, rest = [gathered[:, :step]], gathered[:, step:]
        places, place = jnp.zeros((1,), jnp.int32), jnp.ones((1,), jnp.int32)

    in_part = lax.dot_general(proj_in, layer_in, (((0,), (1,)), ((), ())), preferred_element_type=jnp.float32)
    in_sum = sum_over(in_part, "tensor", tensor)
    seg = segment_ids.reshape(-1)
    inside = jnp.concatenate([jnp.where(seg[None, :] == n, in_sum, 0.0) for n in range(EX_DEV)])
    bank, pick = whole_bank(query_bank, query_ids, sizes["dp"])
    stored = bank.shape[0]
    bank = bank.reshape(stored, width, width).swapaxes(1, 2).reshape(stored, width * width)
    proj = jnp.concatenate([proj_out, proj_out], axis=1)

    total = hidden_sum(parts, places, down_weight)
    scores = last_scores(rest, place, down_weight, total, gate_pre, proj, inside, bank, pick, scale)
    scores = sum_over(scores, "seq", sizes["seq"])
    return sum_over(scores, "tensor", tensor)


def solution(mesh):
    in_specs = (
        P(("groups", "dp", "seq"), "tensor"),
        P(("groups", "dp", "seq"), "tensor"),
        P(("groups", "dp", "seq"), "tensor"),
        P("tensor", None),
        P("tensor", None),
        P("tensor", None),
        P(("groups", "dp"), "seq"),
        P(("groups", "dp"), None),
        P("groups"),
    )
    out_specs = P(("groups", "dp"), None)
    sizes = {name: mesh.shape[name] for name in mesh.axis_names}
    return jax.shard_map(
        functools.partial(body, sizes), mesh=mesh, in_specs=in_specs, out_specs=out_specs, check_vma=False
    )
```

```python
import functools

import jax
import jax.numpy as jnp
from jax import lax
from jax.experimental import pallas as pl
from jax.experimental.pallas import tpu as pltpu
from jax.sharding import PartitionSpec as P

EX_DEV = 4
TILE = 512
EXACT = lax.Precision.HIGHEST


def after(value, *deps):
    return lax.optimization_barrier((value, *deps))[0]


def sum_over(value, axis, size):
    step = 1
    while step < size:
        value = value + lax.ppermute(value, axis, [(i, i ^ step) for i in range(size)])
        step *= 2
    return value


def tile_of(count):
    return max((t for t in range(128, TILE + 1, 128) if count % t == 0), default=count)


def two_terms(value):
    high = value.astype(jnp.bfloat16)
    return high, (value - high.astype(jnp.float32)).astype(jnp.bfloat16)


IN_VMEM = pl.BlockSpec(memory_space=pltpu.VMEM)
IN_SMEM = pl.BlockSpec(memory_space=pltpu.SMEM)
ANYWHERE = pl.BlockSpec(memory_space=pl.ANY)


def column_copy(weight_ref, place, held_ref, sem_ref, chunk):
    hidden, width = held_ref.shape
    tile = tile_of(hidden)
    rows = pl.ds(pl.multiple_of(chunk * tile, tile), tile)
    return pltpu.make_async_copy(
        weight_ref.at[rows, pl.ds(pl.multiple_of(place * width, width), width)],
        held_ref.at[rows, :],
        sem_ref.at[chunk],
    )


def chunks_of(held_ref):
    return held_ref.shape[0] // tile_of(held_ref.shape[0])


def rows_of(held_ref, chunk):
    tile = tile_of(held_ref.shape[0])
    return pl.ds(pl.multiple_of(chunk * tile, tile), tile)


def hidden_kernel(blocks, has_base, places_ref, weight_ref, *refs):
    parts, refs = refs[:blocks], refs[blocks:]
    base_ref, refs = (refs[0], refs[1:]) if has_base else (None, refs)
    total_ref, mark_ref, kept_ref, refs = refs[0], refs[1], refs[2], refs[3:]
    held, turned, sems, kept_sem = refs[:blocks], refs[blocks : 2 * blocks], refs[2 * blocks : -1], refs[-1]
    chunks = chunks_of(total_ref)

    @pl.loop(0, chunks)
    def _(chunk):
        for k in range(blocks):
            column_copy(weight_ref, places_ref[k], held[k], sems[k], chunk).start()

    @pl.loop(0, chunks if has_base else 0)
    def _(chunk):
        column_copy(weight_ref, places_ref[blocks], kept_ref, kept_sem, chunk).start()

    for part, turn in zip(parts, turned):
        turn[...] = part[...].T
    mark_ref[...] = jnp.zeros_like(mark_ref)

    @pl.loop(0, chunks)
    def _(chunk):
        rows = rows_of(total_ref, chunk)
        total = base_ref[rows, :] if has_base else 0.0
        for k in range(blocks):
            column_copy(weight_ref, places_ref[k], held[k], sems[k], chunk).wait()
            total += jnp.dot(held[k][rows, :], turned[k][...], preferred_element_type=jnp.float32)
        total_ref[rows, :] = total

    @pl.loop(0, chunks if has_base else 0)
    def _(chunk):
        column_copy(weight_ref, places_ref[blocks], kept_ref, kept_sem, chunk).wait()


def held_in_vmem(value):
    return pltpu.with_memory_space_constraint(value, pltpu.VMEM)


def hidden_sum(parts, places, weight, base=None):
    tokens, width = parts[0].shape
    hidden = weight.shape[0]
    blocks = len(parts)
    bases = [] if base is None else [held_in_vmem(base)]
    kept = (hidden, width) if bases else (8, 128)
    chunks = pltpu.SemaphoreType.DMA((hidden // tile_of(hidden),))
    return pl.pallas_call(
        functools.partial(hidden_kernel, blocks, bool(bases)),
        in_specs=[IN_SMEM, ANYWHERE] + [IN_VMEM] * (blocks + len(bases)),
        out_specs=[IN_VMEM] * 3,
        scratch_shapes=[pltpu.VMEM((hidden, width), weight.dtype)] * blocks
        + [pltpu.VMEM((width, tokens), parts[0].dtype)] * blocks
        + [chunks] * (blocks + 1),
        out_shape=[
            pltpu.VMEM((hidden, tokens), jnp.float32),
            jax.ShapeDtypeStruct((8, 128), jnp.float32),
            pltpu.VMEM(kept, weight.dtype),
        ],
        input_output_aliases={2 + blocks: 0} if bases else {},
        compiler_params=pltpu.CompilerParams(vmem_limit_bytes=(6 + 9 * blocks) << 20),
        cost_estimate=pl.CostEstimate(
            flops=2 * blocks * tokens * width * hidden,
            bytes_accessed=2 * blocks * width * (tokens + hidden),
            transcendentals=0,
        ),
    )(places, weight, *parts, *bases)


def silu(gate):
    gate = gate.astype(jnp.float32)
    return gate / (1.0 + jnp.exp(-gate))


def factor_kernel(gate_ref, factor_ref):
    @pl.loop(0, chunks_of(factor_ref))
    def _(chunk):
        rows = rows_of(factor_ref, chunk)
        factor_ref[rows, :] = silu(gate_ref[:, rows]).T


def factors(gate):
    tokens, hidden = gate.shape
    return pl.pallas_call(
        factor_kernel,
        in_specs=[IN_VMEM],
        out_specs=IN_VMEM,
        out_shape=pltpu.VMEM((hidden, tokens), jnp.float32),
        compiler_params=pltpu.CompilerParams(vmem_limit_bytes=16 << 20),
        cost_estimate=pl.CostEstimate(
            flops=8 * tokens * hidden, bytes_accessed=6 * tokens * hidden, transcendentals=tokens * hidden
        ),
    )(gate)


def term_loop(part_ref, held_ref, total_ref, factor_ref, proj_ref, out_ref, turned, ahead):
    columns = slice(ahead, ahead + part_ref.shape[0])
    turned[...] = part_ref[...].T
    out_ref[...] = jnp.zeros_like(out_ref)

    @pl.loop(0, chunks_of(held_ref))
    def _(chunk):
        rows = rows_of(held_ref, chunk)
        hidden = total_ref[rows, columns] + jnp.dot(
            held_ref[rows, :], turned[...], preferred_element_type=jnp.float32
        )
        up = (hidden * factor_ref[rows, columns]).astype(jnp.bfloat16)
        out_ref[...] += jnp.dot(proj_ref[:, rows], up, preferred_element_type=jnp.float32)


def first_kernel(part_ref, held_ref, total_ref, factor_ref, proj_ref, out_ref, turned):
    term_loop(part_ref, held_ref, total_ref, factor_ref, proj_ref, out_ref, turned, 0)


def first_terms(part, held, total, factor, proj):
    tokens, width = part.shape
    return pl.pallas_call(
        first_kernel,
        in_specs=[IN_VMEM] * 5,
        out_specs=IN_VMEM,
        scratch_shapes=[pltpu.VMEM((width, tokens), part.dtype)],
        out_shape=pltpu.VMEM((proj.shape[0], tokens), jnp.float32),
        compiler_params=pltpu.CompilerParams(vmem_limit_bytes=12 << 20),
        cost_estimate=pl.CostEstimate(
            flops=2 * tokens * width * held.shape[0], bytes_accessed=2 * tokens * width, transcendentals=0
        ),
    )(part, held_in_vmem(held), held_in_vmem(total), held_in_vmem(factor), proj)


def last_kernel(
    scale, part_ref, held_ref, total_ref, factor_ref, proj_ref, first_ref, inside_ref, bank_ref, scores_ref,
    turned, out_ref, rows_ref, flat_ref, pairs_ref,
):
    tokens = part_ref.shape[0]
    ahead = first_ref.shape[1]
    term_loop(part_ref, held_ref, total_ref, factor_ref, proj_ref, out_ref, turned, ahead)
    width = out_ref.shape[0]
    for ref, columns in ((first_ref, slice(0, ahead)), (out_ref, slice(ahead, ahead + tokens))):
        high, low = two_terms(ref[...])
        rows_ref[:width, columns] = high
        rows_ref[width:, columns] = low
    sketch = jnp.dot(rows_ref[...], inside_ref[0], preferred_element_type=jnp.float32)
    sketch = sketch[:width] + sketch[width:]
    sketch += jnp.dot(rows_ref[:width], inside_ref[1], preferred_element_type=jnp.float32)
    for n in range(0, EX_DEV, 2):
        pairs_ref[n // 2 * width : (n // 2 + 1) * width] = sketch[:, n * width : (n + 2) * width]
    half = width // 2
    left = lax.broadcasted_iota(jnp.int32, (half, 2 * width), 1) < width
    for n in range(0, EX_DEV, 2):
        even = pairs_ref[pl.ds(n * half, half, stride=2), :]
        odd = pairs_ref[pl.ds(n * half + 1, half, stride=2), :]
        flat_ref[n * half : (n + 1) * half] = jnp.where(left, even, pltpu.roll(odd, width, 1))
        flat_ref[(n + 1) * half : (n + 2) * half] = jnp.where(left, pltpu.roll(even, width, 1), odd)
    flat = jnp.concatenate([flat_ref[pl.ds(p, EX_DEV, stride=half), :] for p in range(half)], axis=1)
    bank = bank_ref[...]
    found = sum(jnp.dot(t, bank, preferred_element_type=jnp.float32) for t in two_terms(flat))
    scores_ref[...] = scale * found


def last_scores(part, held, total, factor, proj, first, inside, bank, scale):
    tokens, width = part.shape
    hidden = held.shape[0]
    factors = proj.shape[0]
    return pl.pallas_call(
        functools.partial(last_kernel, scale),
        in_specs=[IN_VMEM] * 8,
        out_specs=IN_VMEM,
        scratch_shapes=[
            pltpu.VMEM((width, tokens), part.dtype),
            pltpu.VMEM((factors, tokens), jnp.float32),
            pltpu.VMEM((2 * factors, inside.shape[1]), jnp.bfloat16),
            pltpu.VMEM((EX_DEV * factors // 2, 2 * factors), jnp.float32),
            pltpu.VMEM((EX_DEV // 2 * factors, 2 * factors), jnp.float32),
        ],
        out_shape=jax.ShapeDtypeStruct((EX_DEV, bank.shape[1]), jnp.float32),
        compiler_params=pltpu.CompilerParams(vmem_limit_bytes=14 << 20),
        cost_estimate=pl.CostEstimate(
            flops=2 * tokens * width * hidden, bytes_accessed=2 * tokens * width, transcendentals=0
        ),
    )(part, *map(held_in_vmem, (held, total, factor)), proj, *map(held_in_vmem, (first, inside, bank)))


def spread_kernel(seg_ref, *refs):
    inside_ref = refs[-1]
    rows = sum(ref[...] for ref in refs[:-1])
    for n in range(EX_DEV):
        columns = slice(n * rows.shape[0], (n + 1) * rows.shape[0])
        high, low = two_terms(jnp.where(seg_ref[...] == n, rows, 0.0).T)
        inside_ref[0, :, columns] = high
        inside_ref[1, :, columns] = low


def spread(segments, *terms):
    width, tokens = terms[0].shape
    return pl.pallas_call(
        spread_kernel,
        out_shape=jax.ShapeDtypeStruct((2, tokens, EX_DEV * width), jnp.bfloat16),
        compiler_params=pltpu.CompilerParams(vmem_limit_bytes=8 << 20),
    )(segments, *terms)


def bank_parts(query_bank, size):
    return [query_bank] + [
        lax.ppermute(query_bank, "dp", [(i, (i + k) % size) for i in range(size)]) for k in range(1, size)
    ]


def picked(parts, query_ids):
    size, held = len(parts), parts[0].shape[0]
    me = lax.axis_index("dp")
    rows = jnp.arange(held, dtype=jnp.int32)
    places = jnp.concatenate([(me - k) % size * held + rows for k in range(size)])
    pick = (places[:, None] == query_ids[None, :]).astype(jnp.bfloat16)
    return lax.dot_general(
        jnp.concatenate(parts), pick, (((0,), (0,)), ((), ())), preferred_element_type=jnp.float32
    ).astype(jnp.bfloat16)


def body(
    sizes, out_grad, layer_in, gate_pre, down_weight, proj_in, proj_out, segment_ids, query_bank, query_ids
):
    tensor = sizes["tensor"]
    me = lax.axis_index("tensor")
    scale = 1.0 / (8.0 * proj_in.shape[1])
    proj = proj_out.T

    send = lambda value, pairs: lax.ppermute(value, "tensor", pairs)
    pick_of = lambda *t: jnp.asarray(t, jnp.int32)[me][None]
    project = lambda rows: lax.dot_general(
        proj_in, rows, (((0,), (1,)), ((), ())), preferred_element_type=jnp.float32
    )

    half = out_grad.shape[0] // 2
    in_part = project(layer_in)
    if tensor == 4:
        pairs, crossed, onward = [(0, 1), (1, 0), (2, 3), (3, 2)], [(0, 3), (3, 0)], [(0, 2), (2, 3), (3, 1), (1, 0)]
        in_near = send(in_part, pairs)
        middle = send(out_grad, [(1, 2), (2, 1), (0, 0), (3, 3)])
        near = send(out_grad, pairs)
        here = after(out_grad, in_part)
        cross = send(here, crossed)
        factor = factors(after(gate_pre, in_part))
        middle = after(middle, factor)
        halves = [middle[:half], middle[half:]]
        in_sum = in_part + after((in_near, in_part), *halves)[0]
        in_rest = send(in_sum, crossed + [(1, 2), (2, 1)])
        far = [send(rows, onward) for rows in halves]
        near, query_bank = after((near, query_bank), in_sum)
        parts = bank_parts(query_bank, sizes["dp"])
        total, mark, _ = hidden_sum([here, near], jnp.concatenate([me[None], me[None] ^ 1]), down_weight)
        bank = picked(after(parts, mark), query_ids)
        cross = after(cross, bank)
        rest = jnp.where((me == 0) | (me == 3), cross, middle)
        places = jnp.concatenate([pick_of(3, 2, 1, 0), pick_of(2, 3, 0, 1)])
        total, mark, held = hidden_sum([rest], places, down_weight, total)
        far[0] = after(far[0], mark)
    else:
        in_sum, in_rest = sum_over(in_part, "tensor", tensor), jnp.zeros_like(in_part)
        factor = factors(gate_pre)
        gathered = lax.all_gather(out_grad, "tensor", axis=1, tiled=True)
        step = gathered.shape[1] // 4
        blocks = [gathered[:, k * step : (k + 1) * step] for k in range(4)]
        far = [blocks[3][:half], blocks[3][half:]]
        places = jnp.arange(4, dtype=jnp.int32)
        total, _, _ = hidden_sum(blocks[:2], places[:2], down_weight)
        total, _, held = hidden_sum(blocks[2:3], places[2:], down_weight, total)
        bank = picked(bank_parts(query_bank, sizes["dp"]), query_ids)

    first = first_terms(far[0], held, total, factor, proj)
    inside = spread(segment_ids, in_sum, after(in_rest, first))
    scores = last_scores(far[1], held, total, factor, proj, first, inside, bank, scale)
    scores = sum_over(scores, "seq", sizes["seq"])
    return sum_over(scores, "tensor", tensor)


def solution(mesh):
    in_specs = (
        P(("groups", "dp", "seq"), "tensor"),
        P(("groups", "dp", "seq"), "tensor"),
        P(("groups", "dp", "seq"), "tensor"),
        P("tensor", None),
        P("tensor", None),
        P("tensor", None),
        P(("groups", "dp"), "seq"),
        P(("groups", "dp"), None),
        P("groups"),
    )
    out_specs = P(("groups", "dp"), None)
    sizes = {name: mesh.shape[name] for name in mesh.axis_names}
    return jax.shard_map(
        functools.partial(body, sizes), mesh=mesh, in_specs=in_specs, out_specs=out_specs, check_vma=False
    )
```

```python
import functools

import jax
import jax.numpy as jnp
from jax import lax
from jax.experimental import pallas as pl
from jax.experimental.pallas import tpu as pltpu
from jax.sharding import PartitionSpec as P

EX_DEV = 4
TILE = 512
EXACT = lax.Precision.HIGHEST


def after(value, *deps):
    return lax.optimization_barrier((value, *deps))[0]


def sum_over(value, axis, size):
    step = 1
    while step < size:
        value = value + lax.ppermute(value, axis, [(i, i ^ step) for i in range(size)])
        step *= 2
    return value


def tile_of(count):
    return max((t for t in range(128, TILE + 1, 128) if count % t == 0), default=count)


def two_terms(value):
    high = value.astype(jnp.bfloat16)
    return high, (value - high.astype(jnp.float32)).astype(jnp.bfloat16)


IN_VMEM = pl.BlockSpec(memory_space=pltpu.VMEM)
IN_SMEM = pl.BlockSpec(memory_space=pltpu.SMEM)
ANYWHERE = pl.BlockSpec(memory_space=pl.ANY)


def column_copy(weight_ref, place, held_ref, sem_ref, chunk):
    hidden, width = held_ref.shape
    tile = tile_of(hidden)
    rows = pl.ds(pl.multiple_of(chunk * tile, tile), tile)
    return pltpu.make_async_copy(
        weight_ref.at[rows, pl.ds(pl.multiple_of(place * width, width), width)],
        held_ref.at[rows, :],
        sem_ref.at[chunk],
    )


def chunks_of(held_ref):
    return held_ref.shape[0] // tile_of(held_ref.shape[0])


def rows_of(held_ref, chunk):
    tile = tile_of(held_ref.shape[0])
    return pl.ds(pl.multiple_of(chunk * tile, tile), tile)


def hidden_kernel(blocks, has_base, places_ref, weight_ref, *refs):
    parts, refs = refs[:blocks], refs[blocks:]
    base_ref, refs = (refs[0], refs[1:]) if has_base else (None, refs)
    total_ref, mark_ref, kept_ref, refs = refs[0], refs[1], refs[2], refs[3:]
    held, turned, sems, kept_sem = refs[:blocks], refs[blocks : 2 * blocks], refs[2 * blocks : -1], refs[-1]
    chunks = chunks_of(total_ref)

    @pl.loop(0, chunks)
    def _(chunk):
        for k in range(blocks):
            column_copy(weight_ref, places_ref[k], held[k], sems[k], chunk).start()

    @pl.loop(0, chunks if has_base else 0)
    def _(chunk):
        column_copy(weight_ref, places_ref[blocks], kept_ref, kept_sem, chunk).start()

    for part, turn in zip(parts, turned):
        turn[...] = part[...].T
    mark_ref[...] = jnp.zeros_like(mark_ref)

    @pl.loop(0, chunks, unroll=True)
    def _(chunk):
        rows = rows_of(total_ref, chunk)
        total = base_ref[rows, :] if has_base else 0.0
        for k in range(blocks):
            column_copy(weight_ref, places_ref[k], held[k], sems[k], chunk).wait()
            total += jnp.dot(held[k][rows, :], turned[k][...], preferred_element_type=jnp.float32)
        total_ref[rows, :] = total

    @pl.loop(0, chunks if has_base else 0)
    def _(chunk):
        column_copy(weight_ref, places_ref[blocks], kept_ref, kept_sem, chunk).wait()


def held_in_vmem(value):
    return pltpu.with_memory_space_constraint(value, pltpu.VMEM)


def hidden_sum(parts, places, weight, base=None):
    tokens, width = parts[0].shape
    hidden = weight.shape[0]
    blocks = len(parts)
    bases = [] if base is None else [held_in_vmem(base)]
    kept = (hidden, width) if bases else (8, 128)
    chunks = pltpu.SemaphoreType.DMA((hidden // tile_of(hidden),))
    return pl.pallas_call(
        functools.partial(hidden_kernel, blocks, bool(bases)),
        in_specs=[IN_SMEM, ANYWHERE] + [IN_VMEM] * (blocks + len(bases)),
        out_specs=[IN_VMEM] * 3,
        scratch_shapes=[pltpu.VMEM((hidden, width), weight.dtype)] * blocks
        + [pltpu.VMEM((width, tokens), parts[0].dtype)] * blocks
        + [chunks] * (blocks + 1),
        out_shape=[
            pltpu.VMEM((hidden, tokens), jnp.float32),
            jax.ShapeDtypeStruct((8, 128), jnp.float32),
            pltpu.VMEM(kept, weight.dtype),
        ],
        input_output_aliases={2 + blocks: 0} if bases else {},
        compiler_params=pltpu.CompilerParams(vmem_limit_bytes=(6 + 9 * blocks) << 20),
        cost_estimate=pl.CostEstimate(
            flops=2 * blocks * tokens * width * hidden,
            bytes_accessed=2 * blocks * width * (tokens + hidden),
            transcendentals=0,
        ),
    )(places, weight, *parts, *bases)


def silu(gate):
    gate = gate.astype(jnp.float32)
    return gate / (1.0 + jnp.exp(-gate))


def factor_kernel(gate_ref, factor_ref):
    @pl.loop(0, chunks_of(factor_ref))
    def _(chunk):
        rows = rows_of(factor_ref, chunk)
        factor_ref[rows, :] = silu(gate_ref[:, rows]).T


def factors(gate):
    tokens, hidden = gate.shape
    return pl.pallas_call(
        factor_kernel,
        in_specs=[IN_VMEM],
        out_specs=IN_VMEM,
        out_shape=pltpu.VMEM((hidden, tokens), jnp.float32),
        compiler_params=pltpu.CompilerParams(vmem_limit_bytes=16 << 20),
        cost_estimate=pl.CostEstimate(
            flops=8 * tokens * hidden, bytes_accessed=6 * tokens * hidden, transcendentals=tokens * hidden
        ),
    )(gate)


def term_loop(part_ref, held_ref, total_ref, factor_ref, proj_ref, out_ref, turned, ahead):
    columns = slice(ahead, ahead + part_ref.shape[0])
    turned[...] = part_ref[...].T
    out_ref[...] = jnp.zeros_like(out_ref)

    @pl.loop(0, chunks_of(held_ref), unroll=True)
    def _(chunk):
        rows = rows_of(held_ref, chunk)
        hidden = total_ref[rows, columns] + jnp.dot(
            held_ref[rows, :], turned[...], preferred_element_type=jnp.float32
        )
        up = (hidden * factor_ref[rows, columns]).astype(jnp.bfloat16)
        out_ref[...] += jnp.dot(proj_ref[:, rows], up, preferred_element_type=jnp.float32)


def first_kernel(part_ref, held_ref, total_ref, factor_ref, proj_ref, out_ref, turned):
    term_loop(part_ref, held_ref, total_ref, factor_ref, proj_ref, out_ref, turned, 0)


def first_terms(part, held, total, factor, proj):
    tokens, width = part.shape
    return pl.pallas_call(
        first_kernel,
        in_specs=[IN_VMEM] * 5,
        out_specs=IN_VMEM,
        scratch_shapes=[pltpu.VMEM((width, tokens), part.dtype)],
        out_shape=pltpu.VMEM((proj.shape[0], tokens), jnp.float32),
        compiler_params=pltpu.CompilerParams(vmem_limit_bytes=12 << 20),
        cost_estimate=pl.CostEstimate(
            flops=2 * tokens * width * held.shape[0], bytes_accessed=2 * tokens * width, transcendentals=0
        ),
    )(*map(held_in_vmem, (part, held, total, factor, proj)))


def last_kernel(
    scale, part_ref, held_ref, total_ref, factor_ref, proj_ref, first_ref, inside_ref, bank_ref, scores_ref,
    turned, out_ref, rows_ref, flat_ref, pairs_ref,
):
    tokens = part_ref.shape[0]
    ahead = first_ref.shape[1]
    term_loop(part_ref, held_ref, total_ref, factor_ref, proj_ref, out_ref, turned, ahead)
    width = out_ref.shape[0]
    for ref, columns in ((first_ref, slice(0, ahead)), (out_ref, slice(ahead, ahead + tokens))):
        high, low = two_terms(ref[...])
        rows_ref[:width, columns] = high
        rows_ref[width:, columns] = low
    sketch = jnp.dot(rows_ref[...], inside_ref[0], preferred_element_type=jnp.float32)
    sketch = sketch[:width] + sketch[width:]
    sketch += jnp.dot(rows_ref[:width], inside_ref[1], preferred_element_type=jnp.float32)
    for n in range(0, EX_DEV, 2):
        pairs_ref[n // 2 * width : (n // 2 + 1) * width] = sketch[:, n * width : (n + 2) * width]
    half = width // 2
    left = lax.broadcasted_iota(jnp.int32, (half, 2 * width), 1) < width
    for n in range(0, EX_DEV, 2):
        even = pairs_ref[pl.ds(n * half, half, stride=2), :]
        odd = pairs_ref[pl.ds(n * half + 1, half, stride=2), :]
        flat_ref[n * half : (n + 1) * half] = jnp.where(left, even, pltpu.roll(odd, width, 1))
        flat_ref[(n + 1) * half : (n + 2) * half] = jnp.where(left, pltpu.roll(even, width, 1), odd)
    flat = jnp.concatenate([flat_ref[pl.ds(p, EX_DEV, stride=half), :] for p in range(half)], axis=1)
    bank = bank_ref[...]
    found = sum(jnp.dot(t, bank, preferred_element_type=jnp.float32) for t in two_terms(flat))
    scores_ref[...] = scale * found


def last_scores(part, held, total, factor, proj, first, inside, bank, scale):
    tokens, width = part.shape
    hidden = held.shape[0]
    factors = proj.shape[0]
    return pl.pallas_call(
        functools.partial(last_kernel, scale),
        in_specs=[IN_VMEM] * 8,
        out_specs=IN_VMEM,
        scratch_shapes=[
            pltpu.VMEM((width, tokens), part.dtype),
            pltpu.VMEM((factors, tokens), jnp.float32),
            pltpu.VMEM((2 * factors, inside.shape[1]), jnp.bfloat16),
            pltpu.VMEM((EX_DEV * factors // 2, 2 * factors), jnp.float32),
            pltpu.VMEM((EX_DEV // 2 * factors, 2 * factors), jnp.float32),
        ],
        out_shape=jax.ShapeDtypeStruct((EX_DEV, bank.shape[1]), jnp.float32),
        compiler_params=pltpu.CompilerParams(vmem_limit_bytes=14 << 20),
        cost_estimate=pl.CostEstimate(
            flops=2 * tokens * width * hidden, bytes_accessed=2 * tokens * width, transcendentals=0
        ),
    )(*map(held_in_vmem, (part, held, total, factor, proj, first, inside, bank)))


def spread_kernel(seg_ref, *refs):
    inside_ref = refs[-1]
    rows = sum(ref[...].astype(jnp.float32) for ref in refs[:-1])
    for n in range(EX_DEV):
        columns = slice(n * rows.shape[0], (n + 1) * rows.shape[0])
        high, low = two_terms(jnp.where(seg_ref[...] == n, rows, 0.0).T)
        inside_ref[0, :, columns] = high
        inside_ref[1, :, columns] = low


def spread(segments, *terms):
    width, tokens = terms[0].shape
    return pl.pallas_call(
        spread_kernel,
        out_shape=jax.ShapeDtypeStruct((2, tokens, EX_DEV * width), jnp.bfloat16),
        compiler_params=pltpu.CompilerParams(vmem_limit_bytes=8 << 20),
    )(segments, *terms)


def bank_parts(query_bank, size):
    return [query_bank] + [
        lax.ppermute(query_bank, "dp", [(i, (i + k) % size) for i in range(size)]) for k in range(1, size)
    ]


def picked(parts, query_ids):
    size, held = len(parts), parts[0].shape[0]
    me = lax.axis_index("dp")
    rows = jnp.arange(held, dtype=jnp.int32)
    places = jnp.concatenate([(me - k) % size * held + rows for k in range(size)])
    pick = (places[:, None] == query_ids[None, :]).astype(jnp.bfloat16)
    return lax.dot_general(
        jnp.concatenate(parts), pick, (((0,), (0,)), ((), ())), preferred_element_type=jnp.float32
    ).astype(jnp.bfloat16)


def body(
    sizes, out_grad, layer_in, gate_pre, down_weight, proj_in, proj_out, segment_ids, query_bank, query_ids
):
    tensor = sizes["tensor"]
    me = lax.axis_index("tensor")
    scale = 1.0 / (8.0 * proj_in.shape[1])
    proj = proj_out.T

    send = lambda value, pairs: lax.ppermute(value, "tensor", pairs)
    short = lambda value: value.astype(jnp.bfloat16)
    pick_of = lambda *t: jnp.asarray(t, jnp.int32)[me][None]
    project = lambda rows: lax.dot_general(
        proj_in, rows, (((0,), (1,)), ((), ())), preferred_element_type=jnp.float32
    )

    half = out_grad.shape[0] // 2
    in_part = project(layer_in)
    if tensor == 4:
        pairs, crossed, onward = [(0, 1), (1, 0), (2, 3), (3, 2)], [(0, 3), (3, 0)], [(0, 2), (2, 3), (3, 1), (1, 0)]
        in_near = send(short(in_part), pairs)
        middle = send(out_grad, [(1, 2), (2, 1), (0, 0), (3, 3)])
        near = send(out_grad, pairs)
        here = after(out_grad, in_part)
        cross = send(here, crossed)
        factor = factors(after(gate_pre, in_part))
        middle = after(middle, factor)
        halves = [middle[:half], middle[half:]]
        in_sum = in_part + after(in_near, *halves).astype(jnp.float32)
        in_rest = send(short(in_sum), crossed + [(1, 2), (2, 1)])
        halves[1] = after(halves[1], in_sum)
        far = [send(rows, onward) for rows in halves]
        near, query_bank = after((near, query_bank), in_sum)
        parts = bank_parts(query_bank, sizes["dp"])
        total, mark, _ = hidden_sum([here, near], jnp.concatenate([me[None], me[None] ^ 1]), down_weight)
        bank = picked(after(parts, mark), query_ids)
        cross = after(cross, bank)
        rest = jnp.where((me == 0) | (me == 3), cross, middle)
        places = jnp.concatenate([pick_of(3, 2, 1, 0), pick_of(2, 3, 0, 1)])
        total, mark, held = hidden_sum([rest], places, down_weight, total)
        far[0] = after(far[0], mark)
    else:
        in_sum, in_rest = sum_over(in_part, "tensor", tensor), jnp.zeros_like(in_part)
        factor = factors(gate_pre)
        gathered = lax.all_gather(out_grad, "tensor", axis=1, tiled=True)
        step = gathered.shape[1] // 4
        blocks = [gathered[:, k * step : (k + 1) * step] for k in range(4)]
        far = [blocks[3][:half], blocks[3][half:]]
        places = jnp.arange(4, dtype=jnp.int32)
        total, _, _ = hidden_sum(blocks[:2], places[:2], down_weight)
        total, _, held = hidden_sum(blocks[2:3], places[2:], down_weight, total)
        bank = picked(bank_parts(query_bank, sizes["dp"]), query_ids)

    first = first_terms(far[0], held, total, factor, proj)
    inside = spread(segment_ids, in_sum, after(in_rest, first))
    scores = last_scores(far[1], held, total, factor, proj, first, inside, bank, scale)
    scores = sum_over(scores, "seq", sizes["seq"])
    return sum_over(scores, "tensor", tensor)


def solution(mesh):
    in_specs = (
        P(("groups", "dp", "seq"), "tensor"),
        P(("groups", "dp", "seq"), "tensor"),
        P(("groups", "dp", "seq"), "tensor"),
        P("tensor", None),
        P("tensor", None),
        P("tensor", None),
        P(("groups", "dp"), "seq"),
        P(("groups", "dp"), None),
        P("groups"),
    )
    out_specs = P(("groups", "dp"), None)
    sizes = {name: mesh.shape[name] for name in mesh.axis_names}
    return jax.shard_map(
        functools.partial(body, sizes), mesh=mesh, in_specs=in_specs, out_specs=out_specs, check_vma=False
    )
```

```python
import functools

import jax
import jax.numpy as jnp
from jax import lax
from jax.experimental import pallas as pl
from jax.experimental.pallas import tpu as pltpu
from jax.sharding import PartitionSpec as P

EX_DEV = 4
COST = 2
TILE = 512
EXACT = lax.Precision.HIGHEST


def after(value, *deps):
    return lax.optimization_barrier((value, *deps))[0]


def sum_over(value, axis, size):
    step = 1
    while step < size:
        value = value + lax.ppermute(value, axis, [(i, i ^ step) for i in range(size)])
        step *= 2
    return value


def tile_of(count):
    return max((t for t in range(128, TILE + 1, 128) if count % t == 0), default=count)


def two_terms(value):
    high = value.astype(jnp.bfloat16)
    return high, (value - high.astype(jnp.float32)).astype(jnp.bfloat16)


IN_VMEM = pl.BlockSpec(memory_space=pltpu.VMEM)
IN_SMEM = pl.BlockSpec(memory_space=pltpu.SMEM)
IN_HBM = pl.BlockSpec(memory_space=pltpu.HBM)


def column_copy(weight_ref, place, held_ref, sem_ref, chunk):
    hidden, width = held_ref.shape
    tile = tile_of(hidden)
    rows = pl.ds(pl.multiple_of(chunk * tile, tile), tile)
    return pltpu.make_async_copy(
        weight_ref.at[rows, pl.ds(pl.multiple_of(place * width, width), width)],
        held_ref.at[rows, :],
        sem_ref.at[chunk],
    )


def chunks_of(held_ref):
    return held_ref.shape[0] // tile_of(held_ref.shape[0])


def rows_of(held_ref, chunk):
    tile = tile_of(held_ref.shape[0])
    return pl.ds(pl.multiple_of(chunk * tile, tile), tile)


def hidden_kernel(blocks, has_base, keeps, places_ref, weight_ref, *refs):
    parts, refs = refs[:blocks], refs[blocks:]
    base_ref, refs = (refs[0], refs[1:]) if has_base else (None, refs)
    total_ref, mark_ref, kept_ref, refs = refs[0], refs[1], refs[2], refs[3:]
    held, turned, sems, kept_sem = refs[:blocks], refs[blocks : 2 * blocks], refs[2 * blocks : -1], refs[-1]
    chunks = chunks_of(total_ref)

    @pl.loop(0, chunks)
    def _(chunk):
        for k in range(blocks):
            column_copy(weight_ref, places_ref[k], held[k], sems[k], chunk).start()

    @pl.loop(0, chunks if keeps else 0)
    def _(chunk):
        column_copy(weight_ref, places_ref[blocks], kept_ref, kept_sem, chunk).start()

    for part, turn in zip(parts, turned):
        turn[...] = part[...].T
    mark_ref[...] = jnp.zeros_like(mark_ref)

    @pl.loop(0, chunks, unroll=True)
    def _(chunk):
        rows = rows_of(total_ref, chunk)
        total = base_ref[rows, :] if has_base else 0.0
        for k in range(blocks):
            column_copy(weight_ref, places_ref[k], held[k], sems[k], chunk).wait()
            total += jnp.dot(held[k][rows, :], turned[k][...], preferred_element_type=jnp.float32)
        total_ref[rows, :] = total

    @pl.loop(0, chunks if keeps else 0)
    def _(chunk):
        column_copy(weight_ref, places_ref[blocks], kept_ref, kept_sem, chunk).wait()


def held_in_vmem(value):
    return pltpu.with_memory_space_constraint(value, pltpu.VMEM)


def hidden_sum(parts, places, weight, base=None, keeps=False):
    tokens, width = parts[0].shape
    hidden = weight.shape[0]
    blocks = len(parts)
    bases = [] if base is None else [held_in_vmem(base)]
    kept = (hidden, width) if keeps else (8, 128)
    chunks = pltpu.SemaphoreType.DMA((hidden // tile_of(hidden),))
    return pl.pallas_call(
        functools.partial(hidden_kernel, blocks, bool(bases), keeps),
        in_specs=[IN_SMEM, IN_HBM] + [IN_VMEM] * (blocks + len(bases)),
        out_specs=[IN_VMEM] * 3,
        scratch_shapes=[pltpu.VMEM((hidden, width), weight.dtype)] * blocks
        + [pltpu.VMEM((width, tokens), parts[0].dtype)] * blocks
        + [chunks] * (blocks + 1),
        out_shape=[
            pltpu.VMEM((hidden, tokens), jnp.float32),
            jax.ShapeDtypeStruct((8, 128), jnp.float32),
            pltpu.VMEM(kept, weight.dtype),
        ],
        input_output_aliases={2 + blocks: 0} if bases else {},
        compiler_params=pltpu.CompilerParams(vmem_limit_bytes=(6 + 9 * blocks) << 20),
        cost_estimate=pl.CostEstimate(
            flops=int(COST * blocks * tokens * width * hidden),
            bytes_accessed=int(COST * blocks * width * (tokens + hidden)),
            transcendentals=0,
        ),
    )(places, pltpu.with_memory_space_constraint(weight, pltpu.HBM), *parts, *bases)


def silu(gate):
    gate = gate.astype(jnp.float32)
    return gate / (1.0 + jnp.exp(-gate))


def factor_kernel(gate_ref, factor_ref):
    @pl.loop(0, chunks_of(factor_ref))
    def _(chunk):
        rows = rows_of(factor_ref, chunk)
        factor_ref[rows, :] = silu(gate_ref[:, rows]).T


def factors(gate):
    tokens, hidden = gate.shape
    return pl.pallas_call(
        factor_kernel,
        in_specs=[IN_VMEM],
        out_specs=IN_VMEM,
        out_shape=pltpu.VMEM((hidden, tokens), jnp.float32),
        compiler_params=pltpu.CompilerParams(vmem_limit_bytes=16 << 20),
        cost_estimate=pl.CostEstimate(
            flops=8 * tokens * hidden, bytes_accessed=6 * tokens * hidden, transcendentals=tokens * hidden
        ),
    )(gate)


def term_loop(part_ref, held_ref, total_ref, factor_ref, proj_ref, out_ref, turned, ahead):
    columns = slice(ahead, ahead + part_ref.shape[0])
    turned[...] = part_ref[...].T
    out_ref[...] = jnp.zeros_like(out_ref)

    @pl.loop(0, chunks_of(held_ref), unroll=True)
    def _(chunk):
        rows = rows_of(held_ref, chunk)
        hidden = total_ref[rows, columns] + jnp.dot(
            held_ref[rows, :], turned[...], preferred_element_type=jnp.float32
        )
        up = (hidden * factor_ref[rows, columns]).astype(jnp.bfloat16)
        out_ref[...] += jnp.dot(proj_ref[:, rows], up, preferred_element_type=jnp.float32)


def first_kernel(*refs):
    term_loop(*refs, 0)


def first_terms(part, held, total, factor, proj):
    tokens, width = part.shape
    return pl.pallas_call(
        first_kernel,
        in_specs=[IN_VMEM] * 5,
        out_specs=IN_VMEM,
        scratch_shapes=[pltpu.VMEM((width, tokens), part.dtype)],
        out_shape=pltpu.VMEM((proj.shape[0], tokens), jnp.float32),
        compiler_params=pltpu.CompilerParams(vmem_limit_bytes=12 << 20),
        cost_estimate=pl.CostEstimate(
            flops=2 * tokens * width * held.shape[0], bytes_accessed=2 * tokens * width, transcendentals=0
        ),
    )(*map(held_in_vmem, (part, held, total, factor, proj)))


def last_kernel(
    scale, part_ref, held_ref, total_ref, factor_ref, proj_ref, first_ref, inside_ref, bank_ref, scores_ref,
    turned, out_ref, rows_ref, flat_ref, pairs_ref,
):
    tokens = part_ref.shape[0]
    ahead = first_ref.shape[1]
    term_loop(part_ref, held_ref, total_ref, factor_ref, proj_ref, out_ref, turned, ahead)
    width = out_ref.shape[0]
    for ref, columns in ((first_ref, slice(0, ahead)), (out_ref, slice(ahead, ahead + tokens))):
        high, low = two_terms(ref[...])
        rows_ref[:width, columns] = high
        rows_ref[width:, columns] = low
    sketch = jnp.dot(rows_ref[...], inside_ref[0], preferred_element_type=jnp.float32)
    sketch = sketch[:width] + sketch[width:]
    sketch += jnp.dot(rows_ref[:width], inside_ref[1], preferred_element_type=jnp.float32)
    for n in range(0, EX_DEV, 2):
        pairs_ref[n // 2 * width : (n // 2 + 1) * width] = sketch[:, n * width : (n + 2) * width]
    half = width // 2
    left = lax.broadcasted_iota(jnp.int32, (half, 2 * width), 1) < width
    for n in range(0, EX_DEV, 2):
        even = pairs_ref[pl.ds(n * half, half, stride=2), :]
        odd = pairs_ref[pl.ds(n * half + 1, half, stride=2), :]
        flat_ref[n * half : (n + 1) * half] = jnp.where(left, even, pltpu.roll(odd, width, 1))
        flat_ref[(n + 1) * half : (n + 2) * half] = jnp.where(left, pltpu.roll(even, width, 1), odd)
    flat = jnp.concatenate([flat_ref[pl.ds(p, EX_DEV, stride=half), :] for p in range(half)], axis=1)
    bank = bank_ref[...]
    found = sum(jnp.dot(t, bank, preferred_element_type=jnp.float32) for t in two_terms(flat))
    scores_ref[...] = scale * found


def last_scores(part, held, total, factor, proj, first, inside, bank, scale):
    tokens, width = part.shape
    hidden = held.shape[0]
    factors = proj.shape[0]
    return pl.pallas_call(
        functools.partial(last_kernel, scale),
        in_specs=[IN_VMEM] * 8,
        out_specs=IN_VMEM,
        scratch_shapes=[
            pltpu.VMEM((width, tokens), part.dtype),
            pltpu.VMEM((factors, tokens), jnp.float32),
            pltpu.VMEM((2 * factors, inside.shape[1]), jnp.bfloat16),
            pltpu.VMEM((EX_DEV * factors // 2, 2 * factors), jnp.float32),
            pltpu.VMEM((EX_DEV // 2 * factors, 2 * factors), jnp.float32),
        ],
        out_shape=jax.ShapeDtypeStruct((EX_DEV, bank.shape[1]), jnp.float32),
        compiler_params=pltpu.CompilerParams(vmem_limit_bytes=14 << 20),
        cost_estimate=pl.CostEstimate(
            flops=2 * tokens * width * hidden, bytes_accessed=2 * tokens * width, transcendentals=0
        ),
    )(*map(held_in_vmem, (part, held, total, factor, proj, first, inside, bank)))


def spread_kernel(seg_ref, *refs):
    inside_ref = refs[-1]
    rows = sum(ref[...].astype(jnp.float32) for ref in refs[:-1])
    for n in range(EX_DEV):
        columns = slice(n * rows.shape[0], (n + 1) * rows.shape[0])
        high, low = two_terms(jnp.where(seg_ref[...] == n, rows, 0.0).T)
        inside_ref[0, :, columns] = high
        inside_ref[1, :, columns] = low


def spread(segments, *terms):
    width, tokens = terms[0].shape
    return pl.pallas_call(
        spread_kernel,
        out_shape=jax.ShapeDtypeStruct((2, tokens, EX_DEV * width), jnp.bfloat16),
        compiler_params=pltpu.CompilerParams(vmem_limit_bytes=8 << 20),
    )(segments, *terms)


def bank_parts(query_bank, size):
    return [query_bank] + [
        lax.ppermute(query_bank, "dp", [(i, (i + k) % size) for i in range(size)]) for k in range(1, size)
    ]


def picked(parts, query_ids):
    size, held = len(parts), parts[0].shape[0]
    me = lax.axis_index("dp")
    rows = jnp.arange(held, dtype=jnp.int32)
    places = jnp.concatenate([(me - k) % size * held + rows for k in range(size)])
    pick = (places[:, None] == query_ids[None, :]).astype(jnp.bfloat16)
    return lax.dot_general(
        jnp.concatenate(parts), pick, (((0,), (0,)), ((), ())), preferred_element_type=jnp.float32
    ).astype(jnp.bfloat16)


def body(
    sizes, out_grad, layer_in, gate_pre, down_weight, proj_in, proj_out, segment_ids, query_bank, query_ids
):
    tensor = sizes["tensor"]
    me = lax.axis_index("tensor")
    scale = 1.0 / (8.0 * proj_in.shape[1])
    proj = proj_out.T

    send = lambda value, pairs: lax.ppermute(value, "tensor", pairs)
    short = lambda value: value.astype(jnp.bfloat16)
    pick_of = lambda *t: jnp.asarray(t, jnp.int32)[me][None]
    project = lambda rows: lax.dot_general(
        proj_in, rows, (((0,), (1,)), ((), ())), preferred_element_type=jnp.float32
    )

    half = out_grad.shape[0] // 2
    in_part = project(layer_in)
    if tensor == 4:
        pairs, onward = [(0, 1), (1, 0), (2, 3), (3, 2)], [(0, 2), (2, 3), (3, 1), (1, 0)]
        in_near = send(short(in_part), pairs)
        inner = send(out_grad, [(1, 2), (2, 1), (0, 0), (3, 3)])
        near = send(out_grad, pairs)
        factor = factors(after(gate_pre, in_part))
        total, mark, _ = hidden_sum([after(out_grad, factor)], me[None], down_weight)
        inner = after(inner, mark)
        halves = [inner[:half], inner[half:]]
        far = [send(rows, onward) for rows in halves]
        in_sum = in_part + after(in_near, *halves).astype(jnp.float32)
        in_rest = send(short(in_sum), [(0, 3), (3, 0), (1, 2), (2, 1)])
        near, query_bank = after((near, query_bank), in_sum)
        parts = bank_parts(query_bank, sizes["dp"])
        total, mark, _ = hidden_sum([near], me[None] ^ 1, down_weight, total)
        far[0] = after(far[0], mark)
        outer = [send(far[0], pairs)]
        far[1] = after(far[1], far[0])
        outer.append(send(far[1], pairs))
        bank = picked(after(parts, far[1]), query_ids)
        places = jnp.concatenate([pick_of(2, 3, 0, 1), pick_of(3, 2, 1, 0)])
        total, mark, held = hidden_sum([jnp.concatenate(far)], places, down_weight, total, True)
        outer[0] = after(outer[0], mark)
    else:
        in_sum, in_rest = sum_over(in_part, "tensor", tensor), jnp.zeros_like(in_part)
        factor = factors(gate_pre)
        gathered = lax.all_gather(out_grad, "tensor", axis=1, tiled=True)
        step = gathered.shape[1] // 4
        blocks = [gathered[:, k * step : (k + 1) * step] for k in range(4)]
        outer = [blocks[3][:half], blocks[3][half:]]
        places = jnp.arange(4, dtype=jnp.int32)
        total, _, _ = hidden_sum(blocks[:2], places[:2], down_weight)
        total, _, held = hidden_sum(blocks[2:3], places[2:], down_weight, total, True)
        bank = picked(bank_parts(query_bank, sizes["dp"]), query_ids)

    first = first_terms(outer[0], held, total, factor, proj)
    inside = spread(segment_ids, in_sum, after(in_rest, first))
    scores = last_scores(outer[1], held, total, factor, proj, first, inside, bank, scale)
    scores = sum_over(scores, "seq", sizes["seq"])
    return sum_over(scores, "tensor", tensor)


def solution(mesh):
    in_specs = (
        P(("groups", "dp", "seq"), "tensor"),
        P(("groups", "dp", "seq"), "tensor"),
        P(("groups", "dp", "seq"), "tensor"),
        P("tensor", None),
        P("tensor", None),
        P("tensor", None),
        P(("groups", "dp"), "seq"),
        P(("groups", "dp"), None),
        P("groups"),
    )
    out_specs = P(("groups", "dp"), None)
    sizes = {name: mesh.shape[name] for name in mesh.axis_names}
    return jax.shard_map(
        functools.partial(body, sizes), mesh=mesh, in_specs=in_specs, out_specs=out_specs, check_vma=False
    )
```

```python
import functools

import jax
import jax.numpy as jnp
from jax import lax
from jax.experimental import pallas as pl
from jax.experimental.pallas import tpu as pltpu
from jax.sharding import PartitionSpec as P

EX_DEV = 4
COST = 2
TILE = 512
EXACT = lax.Precision.HIGHEST


def after(value, *deps):
    return lax.optimization_barrier((value, *deps))[0]


def sum_over(value, axis, size):
    step = 1
    while step < size:
        value = value + lax.ppermute(value, axis, [(i, i ^ step) for i in range(size)])
        step *= 2
    return value


def tile_of(count):
    return max((t for t in range(128, TILE + 1, 128) if count % t == 0), default=count)


def two_terms(value):
    high = value.astype(jnp.bfloat16)
    return high, (value - high.astype(jnp.float32)).astype(jnp.bfloat16)


IN_VMEM = pl.BlockSpec(memory_space=pltpu.VMEM)
IN_SMEM = pl.BlockSpec(memory_space=pltpu.SMEM)
IN_HBM = pl.BlockSpec(memory_space=pltpu.HBM)


def column_copy(weight_ref, place, held_ref, sem_ref, chunk):
    hidden, width = held_ref.shape
    tile = tile_of(hidden)
    rows = pl.ds(pl.multiple_of(chunk * tile, tile), tile)
    return pltpu.make_async_copy(
        weight_ref.at[rows, pl.ds(pl.multiple_of(place * width, width), width)],
        held_ref.at[rows, :],
        sem_ref.at[chunk],
    )


def chunks_of(held_ref):
    return held_ref.shape[0] // tile_of(held_ref.shape[0])


def rows_of(held_ref, chunk):
    tile = tile_of(held_ref.shape[0])
    return pl.ds(pl.multiple_of(chunk * tile, tile), tile)


def hidden_kernel(blocks, has_base, keeps, places_ref, weight_ref, *refs):
    parts, refs = refs[:blocks], refs[blocks:]
    base_ref, refs = (refs[0], refs[1:]) if has_base else (None, refs)
    total_ref, mark_ref, kept_ref, refs = refs[0], refs[1], refs[2], refs[3:]
    held, turned, sems, kept_sem = refs[:blocks], refs[blocks : 2 * blocks], refs[2 * blocks : -1], refs[-1]
    chunks = chunks_of(total_ref)

    @pl.loop(0, chunks)
    def _(chunk):
        for k in range(blocks):
            column_copy(weight_ref, places_ref[k], held[k], sems[k], chunk).start()

    @pl.loop(0, chunks if keeps else 0)
    def _(chunk):
        column_copy(weight_ref, places_ref[blocks], kept_ref, kept_sem, chunk).start()

    for part, turn in zip(parts, turned):
        turn[...] = part[...].T
    mark_ref[...] = jnp.zeros_like(mark_ref)

    @pl.loop(0, chunks, unroll=True)
    def _(chunk):
        rows = rows_of(total_ref, chunk)
        total = base_ref[rows, :] if has_base else 0.0
        for k in range(blocks):
            column_copy(weight_ref, places_ref[k], held[k], sems[k], chunk).wait()
            total += jnp.dot(held[k][rows, :], turned[k][...], preferred_element_type=jnp.float32)
        total_ref[rows, :] = total

    @pl.loop(0, chunks if keeps else 0)
    def _(chunk):
        column_copy(weight_ref, places_ref[blocks], kept_ref, kept_sem, chunk).wait()


def held_in_vmem(value):
    return pltpu.with_memory_space_constraint(value, pltpu.VMEM)


def hidden_sum(parts, places, weight, base=None, keeps=False):
    tokens, width = parts[0].shape
    hidden = weight.shape[0]
    blocks = len(parts)
    bases = [] if base is None else [held_in_vmem(base)]
    kept = (hidden, width) if keeps else (8, 128)
    chunks = pltpu.SemaphoreType.DMA((hidden // tile_of(hidden),))
    return pl.pallas_call(
        functools.partial(hidden_kernel, blocks, bool(bases), keeps),
        in_specs=[IN_SMEM, IN_HBM] + [IN_VMEM] * (blocks + len(bases)),
        out_specs=[IN_VMEM] * 3,
        scratch_shapes=[pltpu.VMEM((hidden, width), weight.dtype)] * blocks
        + [pltpu.VMEM((width, tokens), parts[0].dtype)] * blocks
        + [chunks] * (blocks + 1),
        out_shape=[
            pltpu.VMEM((hidden, tokens), jnp.float32),
            jax.ShapeDtypeStruct((8, 128), jnp.float32),
            pltpu.VMEM(kept, weight.dtype),
        ],
        input_output_aliases={2 + blocks: 0} if bases else {},
        compiler_params=pltpu.CompilerParams(vmem_limit_bytes=(6 + 9 * blocks) << 20),
        cost_estimate=pl.CostEstimate(
            flops=int(COST * blocks * tokens * width * hidden),
            bytes_accessed=int(COST * blocks * width * (tokens + hidden)),
            transcendentals=0,
        ),
    )(places, pltpu.with_memory_space_constraint(weight, pltpu.HBM), *parts, *bases)


def silu(gate):
    gate = gate.astype(jnp.float32)
    return gate / (1.0 + jnp.exp(-gate))


def factor_kernel(gate_ref, factor_ref):
    @pl.loop(0, chunks_of(factor_ref))
    def _(chunk):
        rows = rows_of(factor_ref, chunk)
        factor_ref[rows, :] = silu(gate_ref[:, rows]).T


def factors(gate):
    tokens, hidden = gate.shape
    return pl.pallas_call(
        factor_kernel,
        in_specs=[IN_VMEM],
        out_specs=IN_VMEM,
        out_shape=pltpu.VMEM((hidden, tokens), jnp.float32),
        compiler_params=pltpu.CompilerParams(vmem_limit_bytes=16 << 20),
        cost_estimate=pl.CostEstimate(
            flops=8 * tokens * hidden, bytes_accessed=6 * tokens * hidden, transcendentals=tokens * hidden
        ),
    )(gate)


def term_loop(part_ref, held_ref, total_ref, factor_ref, proj_ref, out_ref, turned, ahead):
    columns = slice(ahead, ahead + part_ref.shape[0])
    turned[...] = part_ref[...].T
    out_ref[...] = jnp.zeros_like(out_ref)

    @pl.loop(0, chunks_of(held_ref), unroll=True)
    def _(chunk):
        rows = rows_of(held_ref, chunk)
        hidden = total_ref[rows, columns] + jnp.dot(
            held_ref[rows, :], turned[...], preferred_element_type=jnp.float32
        )
        up = (hidden * factor_ref[rows, columns]).astype(jnp.bfloat16)
        out_ref[...] += jnp.dot(proj_ref[:, rows], up, preferred_element_type=jnp.float32)


def first_kernel(*refs):
    term_loop(*refs, 0)


def first_terms(part, held, total, factor, proj):
    tokens, width = part.shape
    return pl.pallas_call(
        first_kernel,
        in_specs=[IN_VMEM] * 5,
        out_specs=IN_VMEM,
        scratch_shapes=[pltpu.VMEM((width, tokens), part.dtype)],
        out_shape=pltpu.VMEM((proj.shape[0], tokens), jnp.float32),
        compiler_params=pltpu.CompilerParams(vmem_limit_bytes=12 << 20),
        cost_estimate=pl.CostEstimate(
            flops=2 * tokens * width * held.shape[0], bytes_accessed=2 * tokens * width, transcendentals=0
        ),
    )(*map(held_in_vmem, (part, held, total, factor, proj)))


def last_kernel(
    scale, part_ref, held_ref, total_ref, factor_ref, proj_ref, first_ref, inside_ref, bank_ref, scores_ref,
    turned, out_ref, rows_ref, flat_ref, pairs_ref,
):
    tokens = part_ref.shape[0]
    ahead = first_ref.shape[1]
    term_loop(part_ref, held_ref, total_ref, factor_ref, proj_ref, out_ref, turned, ahead)
    width = out_ref.shape[0]
    for ref, columns in ((first_ref, slice(0, ahead)), (out_ref, slice(ahead, ahead + tokens))):
        high, low = two_terms(ref[...])
        rows_ref[:width, columns] = high
        rows_ref[width:, columns] = low
    sketch = jnp.dot(rows_ref[...], inside_ref[0], preferred_element_type=jnp.float32)
    sketch = sketch[:width] + sketch[width:]
    sketch += jnp.dot(rows_ref[:width], inside_ref[1], preferred_element_type=jnp.float32)
    for n in range(0, EX_DEV, 2):
        pairs_ref[n // 2 * width : (n // 2 + 1) * width] = sketch[:, n * width : (n + 2) * width]
    half = width // 2
    left = lax.broadcasted_iota(jnp.int32, (half, 2 * width), 1) < width
    for n in range(0, EX_DEV, 2):
        even = pairs_ref[pl.ds(n * half, half, stride=2), :]
        odd = pairs_ref[pl.ds(n * half + 1, half, stride=2), :]
        flat_ref[n * half : (n + 1) * half] = jnp.where(left, even, pltpu.roll(odd, width, 1))
        flat_ref[(n + 1) * half : (n + 2) * half] = jnp.where(left, pltpu.roll(even, width, 1), odd)
    flat = jnp.concatenate([flat_ref[pl.ds(p, EX_DEV, stride=half), :] for p in range(half)], axis=1)
    bank = bank_ref[...]
    terms = jnp.concatenate([t.astype(jnp.float32) for t in two_terms(flat)]).astype(jnp.bfloat16)
    found = jnp.dot(terms, bank, preferred_element_type=jnp.float32)
    scores_ref[...] = scale * (found[:EX_DEV] + found[EX_DEV:])


def last_scores(part, held, total, factor, proj, first, inside, bank, scale):
    tokens, width = part.shape
    hidden = held.shape[0]
    factors = proj.shape[0]
    return pl.pallas_call(
        functools.partial(last_kernel, scale),
        in_specs=[IN_VMEM] * 8,
        out_specs=IN_VMEM,
        scratch_shapes=[
            pltpu.VMEM((width, tokens), part.dtype),
            pltpu.VMEM((factors, tokens), jnp.float32),
            pltpu.VMEM((2 * factors, inside.shape[1]), jnp.bfloat16),
            pltpu.VMEM((EX_DEV * factors // 2, 2 * factors), jnp.float32),
            pltpu.VMEM((EX_DEV // 2 * factors, 2 * factors), jnp.float32),
        ],
        out_shape=jax.ShapeDtypeStruct((EX_DEV, bank.shape[1]), jnp.float32),
        compiler_params=pltpu.CompilerParams(vmem_limit_bytes=14 << 20),
        cost_estimate=pl.CostEstimate(
            flops=2 * tokens * width * hidden, bytes_accessed=2 * tokens * width, transcendentals=0
        ),
    )(*map(held_in_vmem, (part, held, total, factor, proj, first, inside, bank)))


def spread_kernel(seg_ref, *refs):
    inside_ref = refs[-1]
    rows = sum(ref[...].astype(jnp.float32) for ref in refs[:-1])
    for n in range(EX_DEV):
        columns = slice(n * rows.shape[0], (n + 1) * rows.shape[0])
        high, low = two_terms(jnp.where(seg_ref[...] == n, rows, 0.0).T)
        inside_ref[0, :, columns] = high
        inside_ref[1, :, columns] = low


def spread(segments, *terms):
    width, tokens = terms[0].shape
    return pl.pallas_call(
        spread_kernel,
        out_shape=jax.ShapeDtypeStruct((2, tokens, EX_DEV * width), jnp.bfloat16),
        compiler_params=pltpu.CompilerParams(vmem_limit_bytes=8 << 20),
    )(segments, *terms)


def bank_parts(query_bank, size):
    return [query_bank] + [
        lax.ppermute(query_bank, "dp", [(i, (i + k) % size) for i in range(size)]) for k in range(1, size)
    ]


def picked(parts, query_ids):
    size, held = len(parts), parts[0].shape[0]
    me = lax.axis_index("dp")
    rows = jnp.arange(held, dtype=jnp.int32)
    places = jnp.concatenate([(me - k) % size * held + rows for k in range(size)])
    pick = (places[:, None] == query_ids[None, :]).astype(jnp.bfloat16)
    return lax.dot_general(
        jnp.concatenate(parts), pick, (((0,), (0,)), ((), ())), preferred_element_type=jnp.float32
    ).astype(jnp.bfloat16)


def body(
    sizes, out_grad, layer_in, gate_pre, down_weight, proj_in, proj_out, segment_ids, query_bank, query_ids
):
    tensor = sizes["tensor"]
    me = lax.axis_index("tensor")
    scale = 1.0 / (8.0 * proj_in.shape[1])
    proj = proj_out.T

    send = lambda value, pairs: lax.ppermute(value, "tensor", pairs)
    short = lambda value: value.astype(jnp.bfloat16)
    pick_of = lambda *t: jnp.asarray(t, jnp.int32)[me][None]
    project = lambda rows: lax.dot_general(
        proj_in, rows, (((0,), (1,)), ((), ())), preferred_element_type=jnp.float32
    )

    half = out_grad.shape[0] // 2
    in_part = project(layer_in)
    if tensor == 4:
        pairs, onward = [(0, 1), (1, 0), (2, 3), (3, 2)], [(0, 2), (2, 3), (3, 1), (1, 0)]
        in_near = send(short(in_part), pairs)
        inner = send(out_grad, [(1, 2), (2, 1), (0, 0), (3, 3)])
        near = send(out_grad, pairs)
        factor = factors(after(gate_pre, in_part))
        total, mark, _ = hidden_sum([after(out_grad, factor)], me[None], down_weight)
        inner = after(inner, mark)
        halves = [inner[:half], inner[half:]]
        far = [send(rows, onward) for rows in halves]
        in_sum = in_part + after(in_near, *halves).astype(jnp.float32)
        in_rest = send(short(in_sum), [(0, 3), (3, 0), (1, 2), (2, 1)])
        near, query_bank = after((near, query_bank), in_sum)
        parts = bank_parts(query_bank, sizes["dp"])
        total, mark, _ = hidden_sum([near], me[None] ^ 1, down_weight, total)
        far[0] = after(far[0], mark)
        outer = [send(far[0], pairs)]
        far[1] = after(far[1], far[0])
        outer.append(send(far[1], pairs))
        bank = picked(after(parts, far[1]), query_ids)
        places = jnp.concatenate([pick_of(2, 3, 0, 1), pick_of(3, 2, 1, 0)])
        total, mark, held = hidden_sum([jnp.concatenate(far)], places, down_weight, total, True)
        outer[0] = after(outer[0], mark)
    else:
        in_sum, in_rest = sum_over(in_part, "tensor", tensor), jnp.zeros_like(in_part)
        factor = factors(gate_pre)
        gathered = lax.all_gather(out_grad, "tensor", axis=1, tiled=True)
        step = gathered.shape[1] // 4
        blocks = [gathered[:, k * step : (k + 1) * step] for k in range(4)]
        outer = [blocks[3][:half], blocks[3][half:]]
        places = jnp.arange(4, dtype=jnp.int32)
        total, _, _ = hidden_sum(blocks[:2], places[:2], down_weight)
        total, _, held = hidden_sum(blocks[2:3], places[2:], down_weight, total, True)
        bank = picked(bank_parts(query_bank, sizes["dp"]), query_ids)

    first = first_terms(outer[0], held, total, factor, proj)
    inside = spread(segment_ids, in_sum, after(in_rest, first))
    scores = last_scores(outer[1], held, total, factor, proj, first, inside, bank, scale)
    scores = sum_over(scores, "seq", sizes["seq"])
    return sum_over(scores, "tensor", tensor)


def solution(mesh):
    in_specs = (
        P(("groups", "dp", "seq"), "tensor"),
        P(("groups", "dp", "seq"), "tensor"),
        P(("groups", "dp", "seq"), "tensor"),
        P("tensor", None),
        P("tensor", None),
        P("tensor", None),
        P(("groups", "dp"), "seq"),
        P(("groups", "dp"), None),
        P("groups"),
    )
    out_specs = P(("groups", "dp"), None)
    sizes = {name: mesh.shape[name] for name in mesh.axis_names}
    return jax.shard_map(
        functools.partial(body, sizes), mesh=mesh, in_specs=in_specs, out_specs=out_specs, check_vma=False
    )
```
